256 devices in a mesh: rep: 4 (over z_hi, core), fsdp: 64 (over x, y, z_lo).
Axes of the slice: x: 4, y: 4, z: 8 (z_hi: 2, z_lo: 4; z = z_hi * 4 + z_lo), core: 2. Of those that a mesh axis runs over, the one named last changes fastest.
Arguments:
- base_weights: float32 [4096, 14336], P('fsdp'), may hold values from -4 to 4
- local_weights: bfloat16 [4, 4096, 14336], P('rep', 'fsdp'), may hold values from -4 to 4
- momentum: float32 [4096, 14336], P('fsdp', 'rep'), may hold values from -3 to 3
- drift_exponent: int32 [4, 4096, 112], P('rep', 'fsdp'), may hold values from -3 to -1
- sum_exponent: int32 [4096, 112], P('fsdp', 'rep'), may hold values from -3 to -1
- blend_ratio: int32 [2], replicated, may hold values from 1 to 8, as said below
Outputs:
- new_base: float32 [4096, 14336], P('fsdp')
- new_momentum: float32 [4096, 14336], P('fsdp', 'rep')
- new_local: bfloat16 [4, 4096, 14336], P('rep', 'fsdp')
The draws below stay inside these ranges and needn't reach their ends.
Inputs may be any that keep to these rules, and one draw needn't show every extreme that they name: blend_ratio[1] is 8 and blend_ratio[0] < blend_ratio[1].
All inputs are finite; a program needn't handle non-finite values.
Results may differ from the reference program's by a relative error of at most 0.0029.
Values may be sent and summed in bfloat16 or wider, within the bound.
No kernel may reach another device: no remote copies, remote signals or barrier semaphores. Data moves between devices by JAX's collectives and lax.ppermute only.
A program may use at most 64 MiB of HBM per device.

```python
import jax
import jax.numpy as jnp
from jax import lax

ROWS = 4096
COLS = 14336
BLOCK = 128
REPLICAS = 4


def shared_raw(key):
    return jnp.clip(jax.random.normal(key, (ROWS, COLS), jnp.float32), -4.0, 4.0)


def draw_base_weights(key, part):
    raw_values = shared_raw(key)
    return jnp.floor(raw_values * 1024.0) / 1024.0


def draw_local_weights(key, part):
    raw_values = shared_raw(key)
    key = jax.random.fold_in(key, 12)
    local_noise = 0.5 * jax.random.normal(key, (REPLICAS, ROWS, COLS), jnp.float32)
    moved = jnp.clip(raw_values[None] + local_noise, -3.9, 3.9)
    return (jnp.floor(moved * 64.0) / 64.0).astype(jnp.bfloat16)


def draw_blend_ratio(key, part):
    key = jax.random.fold_in(key, 13)
    numerator = jax.random.randint(key, (), 1, 8, jnp.int32)
    denominator = jnp.int32(8)
    return jnp.stack([numerator, denominator]).astype(jnp.int32)


def touch_ends(array, rng, smallest, top_value):
    place = [jax.random.randint(jax.random.fold_in(rng, axis), (), 0, length) for axis, length in enumerate(array.shape)]
    main_axis = array.shape.index(max(array.shape))
    beside = place[:main_axis] + [(place[main_axis] + 1) % array.shape[main_axis]] + place[main_axis + 1:]
    return array.at[tuple(place)].set(smallest).at[tuple(beside)].set(top_value)


def block_scale(rng, shape, split, smallest, largest):
    def one(position, shards_of):
        draws = jax.random.uniform(jax.random.fold_in(jax.random.fold_in(rng, 6), position), (shards_of,), jnp.float32, smallest / len(split), largest / len(split))
        return jnp.repeat(jnp.exp(draws), shape[position] // shards_of).reshape((-1,) + (1,) * (len(shape) - position - 1))

    gain = one(*split[0])
    for cut in split[1:]:
        gain = gain * one(*cut)
    return gain


def noise(key, dims, scale, most, shards=(), kind=jnp.bfloat16):
    gain = block_scale(key, dims, shards, -0.22, 0.18) if shards else 1.0
    array = jax.random.normal(key, dims, jnp.float32) * scale * gain
    return jnp.minimum(jnp.maximum(array, -most), most).astype(kind)


def setup_inputs(seed: int = 0) -> dict:
    key_of = jax.random.split(jax.random.key(seed), 7)
    return {
        "base_weights": draw_base_weights(jax.random.fold_in(key_of[6], 71), 0),
        "local_weights": draw_local_weights(jax.random.fold_in(key_of[6], 71), 0),
        "momentum": noise(key_of[2], (ROWS, COLS), 0.5, 3.0, ((0, 64), (1, 4)), jnp.float32),
        "drift_exponent": touch_ends(jax.random.randint(key_of[3], (REPLICAS, ROWS, COLS // BLOCK), -3, 0), jax.random.fold_in(key_of[3], 1), -3, -1).astype(jnp.int32),
        "sum_exponent": touch_ends(jax.random.randint(key_of[4], (ROWS, COLS // BLOCK), -3, 0), jax.random.fold_in(key_of[4], 1), -3, -1).astype(jnp.int32),
        "blend_ratio": draw_blend_ratio(jax.random.fold_in(key_of[6], 71), 0),
    }


momentum_decay = 0.9
outer_rate = 0.7


def block_scales(exponent):
    table = jnp.zeros(exponent.shape, jnp.float32)
    for exponent_value in range(-8, 1):
        table = jnp.where(exponent == exponent_value, jnp.float32(2.0 ** exponent_value), table)
    return table


def block_codes(values, exponent):
    shape = values.shape
    blocks = values.reshape(shape[:-1] + (shape[-1] // BLOCK, BLOCK))
    scales = block_scales(exponent)[..., None]
    levels = jnp.clip(jnp.floor(blocks / scales + 0.5), -8.0, 7.0)
    return (levels * scales).reshape(shape)


def reference(base_weights, local_weights, momentum, drift_exponent, sum_exponent, blend_ratio):
    def add_replica(carry, pair):
        layer, exponent = pair
        drift = base_weights - layer.astype(jnp.float32)
        sent = block_codes(drift, exponent).astype(jnp.bfloat16)
        return carry + sent.astype(jnp.float32), None

    summed, _ = lax.scan(add_replica, jnp.zeros(base_weights.shape, jnp.float32), (local_weights, drift_exponent))
    outer_grad = block_codes(summed / REPLICAS, sum_exponent)
    new_momentum = momentum_decay * momentum + outer_grad
    new_base = base_weights - outer_rate * (outer_grad + momentum_decay * new_momentum)
    share = blend_ratio[0].astype(jnp.float32) / blend_ratio[1].astype(jnp.float32)

    def blend(layer):
        return (share * layer.astype(jnp.float32) + (1.0 - share) * new_base).astype(jnp.bfloat16)

    new_local = lax.map(blend, local_weights)
    return new_base, new_momentum, new_local
```

```python
import functools

import jax
import jax.numpy as jnp
from jax import lax
from jax.experimental import pallas as pl
from jax.experimental.pallas import tpu as pltpu
from jax.sharding import PartitionSpec as P

BLOCK = 128
QUARTER = 28
CHUNKS = (15, 13)
PIECE = 7

VMEM_LIMIT = 12 * 1024 * 1024

momentum_decay = 0.9
outer_rate = 0.7

F32 = jnp.float32
BF16 = jnp.bfloat16
IN_HBM = pl.BlockSpec(memory_space=pltpu.HBM)
ANYWHERE = pl.BlockSpec(memory_space=pl.ANY)
IN_VMEM = pl.BlockSpec(memory_space=pltpu.VMEM)


class Copies:
    def __init__(self, sems):
        self.sems = sems
        self.used = 0

    def start(self, source, target):
        copy = pltpu.make_async_copy(source, target, self.sems.at[self.used])
        self.used += 1
        copy.start()
        return copy


def pieces_of(blocks):
    return [(i, min(PIECE, blocks - i)) for i in range(0, blocks, PIECE)]


def window(quarter, start, count):
    return pl.ds(pl.multiple_of((quarter * QUARTER + start) * BLOCK, BLOCK), count * BLOCK)


def span(start, count):
    return pl.ds(start * BLOCK, count * BLOCK)


def scale_table(exponent):
    rows, blocks = exponent.shape
    if blocks < BLOCK:
        exponent = jnp.concatenate([exponent, jnp.zeros((rows, BLOCK - blocks), jnp.int32)], 1)
    scale = jnp.zeros(exponent.shape, F32)
    inverse = jnp.zeros(exponent.shape, F32)
    for value in range(-8, 1):
        hit = exponent == value
        scale = jnp.where(hit, F32(2.0**value), scale)
        inverse = jnp.where(hit, F32(2.0**-value), inverse)
    return scale, inverse


def rolled(table, first):
    return tuple(pltpu.roll(x, lax.rem(BLOCK - first, BLOCK), 1) for x in table)


def code(values, scales, j):
    scale, inverse = (s[:, j : j + 1] for s in scales)
    return jnp.clip(jnp.floor(values * inverse + 0.5), -8.0, 7.0) * scale


def block(j):
    return slice(j * BLOCK, (j + 1) * BLOCK)


def codes_kernel(parts, n_after, base, local, drift, *refs):
    outs = refs[n_after : n_after + len(parts)]
    base_at, local_at, drift_at, sems = refs[n_after + len(parts) :]
    rep = lax.axis_index("rep")
    copies = Copies(sems)
    exps = copies.start(drift, drift_at)
    arriving = []
    at = 0
    for out, (flip, start, count) in zip(outs, parts):
        for i, n in pieces_of(count):
            cols, here = window(rep ^ flip, start + i, n), span(at, n)
            arriving.append((
                out, i, n, at, (rep ^ flip) * QUARTER + start + i,
                copies.start(base.at[:, cols], base_at.at[:, here]),
                copies.start(local.at[0, :, cols], local_at.at[:, here]),
            ))
            at += n
    exps.wait()
    table = scale_table(drift_at[0])
    for out, i, n, at, first, *group in arriving:
        scales = rolled(table, first)
        for copy in group:
            copy.wait()
        for j in range(n):
            cols = block(at + j)
            drifted = base_at[:, cols] - local_at[:, cols].astype(F32)
            out[:, block(i + j)] = code(drifted, scales, j).astype(BF16)


def pair_kernel(n_after, own, other, *refs):
    out = refs[n_after]
    for j in range(own.shape[1] // BLOCK):
        cols = block(j)
        out[:, cols] = (own[:, cols].astype(F32) + other[:, cols].astype(F32)).astype(BF16)


def update_kernel(start, count, n_others, first, base, local, drift, sums, momentum, share, remote, *refs):
    others, refs = refs[:n_others], refs[n_others:]
    others = [(ref, j) for ref in others for j in range(ref.shape[1] // BLOCK)]
    if not first:
        refs = refs[3:]
    new_base, new_momentum, new_local, sent, kept = refs[:5]
    base_at, local_at, drift_at, sums_at, momentum_at, share_at = refs[5:11]
    out_base, out_momentum, out_local, sems, out_sems = refs[11:]
    quarter = lax.axis_index("rep")
    copies, leaving = Copies(sems), Copies(out_sems)
    small = [copies.start(drift, drift_at), copies.start(sums, sums_at), copies.start(share, share_at)]
    arriving = []
    for i, n in pieces_of(count):
        cols, here = window(quarter, start + i, n), span(i, n)
        arriving.append([
            copies.start(base.at[:, cols], base_at.at[:, here]),
            copies.start(local.at[0, :, cols], local_at.at[:, here]),
            copies.start(momentum.at[:, span(start + i, n)], momentum_at.at[:, here]),
        ])
    for copy in small:
        copy.wait()
    scales = rolled(scale_table(drift_at[0]), quarter * QUARTER + start)
    sum_scales = scale_table(sums_at[...])
    part = share_at[0:1, :]
    outs = []
    for (i, n), group in zip(pieces_of(count), arriving):
        for copy in group:
            copy.wait()
        for j in range(i, i + n):
            cols = block(j)
            old = base_at[:, cols]
            layer = local_at[:, cols].astype(F32)
            own = code(old - layer, scales, j)
            other, at = others[j]
            summed = own + other[:, block(at)].astype(F32) + remote[:, cols].astype(F32)
            outer_grad = code(summed * 0.25, sum_scales, start + j)
            moved = momentum_decay * momentum_at[:, cols] + outer_grad
            value = old - outer_rate * (outer_grad + momentum_decay * moved)
            rounded = value.astype(BF16)
            out_momentum[:, cols] = moved
            kept[:, cols] = value
            sent[:, cols] = rounded
            out_base[:, cols] = rounded.astype(F32)
            out_local[:, cols] = (part * layer + (1.0 - part) * value).astype(BF16)
        cols, here = window(quarter, start + i, n), span(i, n)
        outs += [
            leaving.start(out_base.at[:, here], new_base.at[:, cols]),
            leaving.start(out_momentum.at[:, here], new_momentum.at[:, span(start + i, n)]),
            leaving.start(out_local.at[:, here], new_local.at[0, :, cols]),
        ]
    for copy in outs:
        copy.wait()


def blend_kernel(parts, n_values, local, share, *refs):
    values = refs[:n_values]
    new_base, new_local = refs[n_values + 2 : n_values + 4]
    local_at, share_at, out_base, out_local, sems, out_sems = refs[n_values + 4 :]
    rep = lax.axis_index("rep")
    copies, leaving = Copies(sems), Copies(out_sems)
    shared = copies.start(share, share_at)
    arriving = []
    places = []
    at = 0
    for value, (flip, start, count) in zip(values, parts):
        for i, n in pieces_of(count):
            cols, here = window(rep ^ flip, start + i, n), span(at, n)
            places.append((value, i, at, n, cols, here))
            arriving.append(copies.start(local.at[0, :, cols], local_at.at[:, here]))
            at += n
    shared.wait()
    part = share_at[0:1, :]
    outs = []
    for (value, i, at, n, cols, here), copy in zip(places, arriving):
        copy.wait()
        for j in range(n):
            layer = local_at[:, block(at + j)].astype(F32)
            arrived = value[:, block(i + j)].astype(F32)
            out_base[:, block(at + j)] = arrived.astype(BF16).astype(F32)
            out_local[:, block(at + j)] = (part * layer + (1.0 - part) * arrived).astype(BF16)
        outs += [
            leaving.start(out_base.at[:, here], new_base.at[:, cols]),
            leaving.start(out_local.at[:, here], new_local.at[0, :, cols]),
        ]
    for copy in outs:
        copy.wait()


def on_device(base_weights, local_weights, momentum, drift_exponent, sum_exponent, blend_ratio):
    plain_local = local_weights
    base_weights, local_weights, momentum, drift_exponent = (
        pltpu.with_memory_space_constraint(x, pltpu.HBM)
        for x in (base_weights, local_weights, momentum, drift_exponent)
    )
    rows, cols = base_weights.shape
    owned = momentum.shape[1]
    blocks = drift_exponent.shape[2]
    sum_exponent = jnp.pad(sum_exponent, ((0, 0), (0, BLOCK - sum_exponent.shape[1])))
    share = blend_ratio[0].astype(F32) / blend_ratio[1].astype(F32)
    share = jnp.full((8, BLOCK), share, F32)

    def wide(count, dtype):
        return pltpu.VMEM((rows, count * BLOCK), dtype)

    def sems(n):
        return pltpu.SemaphoreType.DMA((n,))

    def call(body, in_specs, out_specs, out_shape, scratch, name, aliases=None, cost=1):
        return pl.pallas_call(
            body,
            in_specs=in_specs,
            out_specs=out_specs,
            out_shape=out_shape,
            scratch_shapes=scratch,
            input_output_aliases=aliases or {},
            compiler_params=pltpu.CompilerParams(vmem_limit_bytes=VMEM_LIMIT),
            cost_estimate=pl.CostEstimate(flops=1, bytes_accessed=cost, transcendentals=0),
            name=name,
        )

    def codes(parts, after=()):
        count = sum(p[2] for p in parts)
        n = sum(len(pieces_of(p[2])) for p in parts)
        return call(
            functools.partial(codes_kernel, parts, len(after)),
            [IN_HBM] * 3 + [ANYWHERE] * len(after), (IN_VMEM,) * len(parts),
            tuple(jax.ShapeDtypeStruct((rows, p[2] * BLOCK), BF16) for p in parts),
            [wide(count, F32), wide(count, BF16), pltpu.VMEM((1, rows, blocks), jnp.int32), sems(1 + 2 * n)],
            "codes",
        )(base_weights, local_weights, drift_exponent, *after)

    def pair(own, other, after=()):
        return call(
            functools.partial(pair_kernel, len(after)), [IN_VMEM] * 2 + [ANYWHERE] * len(after), IN_VMEM,
            jax.ShapeDtypeStruct(own.shape, BF16), [], "pair",
        )(own, other, *after)

    full = (
        jax.ShapeDtypeStruct((rows, cols), F32),
        jax.ShapeDtypeStruct((rows, owned), F32),
        jax.ShapeDtypeStruct((1, rows, cols), BF16),
    )

    def update(start, count, others, remote, held):
        n = len(pieces_of(count))
        args = [base_weights, local_weights, drift_exponent, sum_exponent, momentum, share, remote, *others]
        specs = [IN_HBM] * 3 + [ANYWHERE] + [IN_HBM] + [ANYWHERE] + [IN_VMEM] * (1 + len(others))
        aliases = {}
        if held is not None:
            aliases = {len(args) + i: i for i in range(3)}
            args += held
            specs += [IN_HBM] * 3
        out = call(
            functools.partial(update_kernel, start, count, len(others), held is None),
            specs, (IN_HBM,) * 3 + (IN_VMEM,) * 2,
            full + (
                jax.ShapeDtypeStruct((rows, count * BLOCK), BF16),
                jax.ShapeDtypeStruct((rows, count * BLOCK), F32),
            ),
            [
                wide(count, F32), wide(count, BF16), pltpu.VMEM((1, rows, blocks), jnp.int32),
                pltpu.VMEM((rows, BLOCK), jnp.int32), wide(count, F32), pltpu.VMEM((8, BLOCK), F32),
                wide(count, F32), wide(count, F32), wide(count, BF16), sems(3 + 3 * n), sems(3 * n),
            ],
            "update", aliases,
        )(*args)
        return list(out[:3]), out[3], out[4]

    def blend(parts, values, held, cost=1):
        count = sum(p[2] for p in parts)
        n = sum(len(pieces_of(p[2])) for p in parts)
        new_base, new_local = call(
            functools.partial(blend_kernel, parts, len(values)),
            [ANYWHERE] * 2 + [IN_VMEM] * len(values) + [IN_HBM] * 2, (IN_HBM, IN_HBM), (full[0], full[2]),
            [
                wide(count, BF16), pltpu.VMEM((8, BLOCK), F32),
                wide(count, F32), wide(count, BF16), sems(1 + n), sems(2 * n),
            ],
            "blend", {2 + len(values): 0, 3 + len(values): 1}, cost,
        )(plain_local, share, *values, held[0], held[2])
        return [new_base, held[1], new_local]

    def to_core(x):
        return lax.ppermute(x, "rep", [(0, 1), (1, 0), (2, 3), (3, 2)])

    def to_chip(x):
        return lax.ppermute(x, "rep", [(0, 2), (2, 0), (1, 3), (3, 1)])

    plan = [(sum(CHUNKS[:i]), CHUNKS[i]) for i in range(len(CHUNKS))]

    (a0, a1), (b0, b1) = plan
    there_first, here_first = codes([(3, a0, a1), (2, a0, a1)])
    there_second, here_second = codes([(3, b0, b1), (2, b0, b1)], after=(there_first,))
    core_first, core_second = to_core(there_first), to_core(there_second)
    pair_first = pair(here_first, core_first, after=(there_second,))
    pair_second = pair(here_second, core_second, after=(pair_first,))
    chip_first, chip_second = to_chip(pair_first), to_chip(pair_second)
    cuts = [(a0, a1 - a1 // 2), (a0 + a1 - a1 // 2, a1 // 2), (b0, b1 - b1 // 2), (b0 + b1 - b1 // 2, b1 // 2)]
    others = [to_core(x) for x in codes([(1, *cut) for cut in cuts], after=(pair_second,))]
    held, sent_first, kept_first = update(a0, a1, others[:2], chip_first, None)
    held, sent_second, kept_second = update(b0, b1, others[2:], chip_second, held)
    far_first, far_second = to_chip(sent_first), to_chip(sent_second)
    near_first, near_second = to_core(kept_first), to_core(kept_second)
    held = blend([(1, a0, a1), (1, b0, b1)], [near_first, near_second], held)
    held = blend([(2, a0, a1), (3, a0, a1)], [far_first, to_core(far_first)], held)
    far_second, held = lax.optimization_barrier((far_second, held))
    forwarded = to_core(far_second)
    held = blend([(2, b0, b1)], [far_second], held)
    held = blend([(3, b0, b1)], [forwarded], held)
    return tuple(held)


def solution(mesh):
    return jax.shard_map(
        on_device,
        mesh=mesh,
        in_specs=(
            P("fsdp", None),
            P("rep", "fsdp", None),
            P("fsdp", "rep"),
            P("rep", "fsdp", None),
            P("fsdp", "rep"),
            P(),
        ),
        out_specs=(P("fsdp", None), P("fsdp", "rep"), P("rep", "fsdp", None)),
        check_vma=False,
    )
```

```python
import functools

import jax
import jax.numpy as jnp
from jax import lax
from jax.experimental import pallas as pl
from jax.experimental.pallas import tpu as pltpu
from jax.sharding import PartitionSpec as P

BLOCK = 128
QUARTER = 28
FIRST, SECOND = 16, 12
BACK_FIRST, BACK_SECOND = 13, 15
AWAY_SECOND = (12,)
CODES = (10, 9, 9)
NEAR_FIRST, NEAR_SECOND = (7, 6), (5, 5, 5)
FORWARD_FIRST = (7, 6)
PIECE = 7
VMEM_LIMIT = 12 * 1024 * 1024

momentum_decay = 0.9
outer_rate = 0.7

F32 = jnp.float32
BF16 = jnp.bfloat16
IN_HBM = pl.BlockSpec(memory_space=pltpu.HBM)
ANYWHERE = pl.BlockSpec(memory_space=pl.ANY)
IN_VMEM = pl.BlockSpec(memory_space=pltpu.VMEM)


class Copies:
    def __init__(self, sems):
        self.sems = sems
        self.used = 0

    def start(self, source, target):
        copy = pltpu.make_async_copy(source, target, self.sems.at[self.used])
        self.used += 1
        copy.start()
        return copy


def pieces_of(blocks):
    return [(i, min(PIECE, blocks - i)) for i in range(0, blocks, PIECE)]


def cut(start, counts):
    return [(start + sum(counts[:i]), count) for i, count in enumerate(counts)]


def window(quarter, start, count):
    return pl.ds(pl.multiple_of((quarter * QUARTER + start) * BLOCK, BLOCK), count * BLOCK)


def span(start, count):
    return pl.ds(start * BLOCK, count * BLOCK)


def block(j):
    return slice(j * BLOCK, (j + 1) * BLOCK)


def places_in(refs):
    return [(ref, j) for ref in refs for j in range(ref.shape[1] // BLOCK)]


def scale_table(exponent):
    rows, blocks = exponent.shape
    if blocks < BLOCK:
        exponent = jnp.concatenate([exponent, jnp.zeros((rows, BLOCK - blocks), jnp.int32)], 1)
    scale = jnp.zeros(exponent.shape, F32)
    inverse = jnp.zeros(exponent.shape, F32)
    for value in range(-8, 1):
        hit = exponent == value
        scale = jnp.where(hit, F32(2.0**value), scale)
        inverse = jnp.where(hit, F32(2.0**-value), inverse)
    return scale, inverse


def rolled(table, first):
    return tuple(pltpu.roll(x, lax.rem(BLOCK - first, BLOCK), 1) for x in table)


def code(values, scales, j):
    scale, inverse = (s[:, j : j + 1] for s in scales)
    return jnp.clip(jnp.floor(values * inverse + 0.5), -8.0, 7.0) * scale


def codes_kernel(parts, n_after, base, local, drift, *refs):
    outs = refs[n_after : n_after + len(parts)]
    base_at, local_at, drift_at, sems = refs[n_after + len(parts) :]
    rep = lax.axis_index("rep")
    copies = Copies(sems)
    exps = copies.start(drift, drift_at)
    arriving = []
    at = 0
    for out, (flip, start, count) in zip(outs, parts):
        for i, n in pieces_of(count):
            cols, here = window(rep ^ flip, start + i, n), span(at, n)
            arriving.append((
                out, i, n, at, (rep ^ flip) * QUARTER + start + i,
                copies.start(base.at[:, cols], base_at.at[:, here]),
                copies.start(local.at[0, :, cols], local_at.at[:, here]),
            ))
            at += n
    exps.wait()
    table = scale_table(drift_at[0])
    for out, i, n, at, first, *group in arriving:
        scales = rolled(table, first)
        for copy in group:
            copy.wait()
        for j in range(n):
            cols = block(at + j)
            drifted = base_at[:, cols] - local_at[:, cols].astype(F32)
            out[:, block(i + j)] = code(drifted, scales, j).astype(BF16)


def pair_kernel(own, *refs):
    *others, out = refs
    for j, (other, at) in enumerate(places_in(others)):
        cols = block(j)
        out[:, cols] = (own[:, cols].astype(F32) + other[:, block(at)].astype(F32)).astype(BF16)


def prepare_kernel(n_others, base, local, drift, momentum, sums, *refs):
    others = places_in(refs[:n_others])
    base_out, momentum_out, held, scale_out, inverse_out, local_at, drift_at, sems = refs[n_others:]
    quarter = lax.axis_index("rep")
    copies = Copies(sems)
    exps = copies.start(drift, drift_at)
    arriving = []
    for i, n in pieces_of(QUARTER):
        cols, here = window(quarter, i, n), span(i, n)
        arriving.append((
            copies.start(base.at[:, cols], base_out.at[:, here]),
            copies.start(local.at[0, :, cols], local_at.at[:, here]),
        ))
    last = copies.start(momentum, momentum_out)
    scale_out[...], inverse_out[...] = scale_table(sums[...])
    exps.wait()
    scales = rolled(scale_table(drift_at[0]), quarter * QUARTER)
    for (i, n), group in zip(pieces_of(QUARTER), arriving):
        for copy in group:
            copy.wait()
        for j in range(i, i + n):
            cols = block(j)
            other, at = others[j]
            own = code(base_out[:, cols] - local_at[:, cols].astype(F32), scales, j)
            held[:, cols] = (own + other[:, block(at)].astype(F32)).astype(BF16)
    last.wait()


def update_kernel(start, count, skip, n_remote, base, momentum, held, scale, inverse, *refs):
    remotes = places_in(refs[:n_remote])[skip:]
    sent, moved_out, *kept = refs[n_remote:]
    kept = places_in(kept)
    scales = scale[...], inverse[...]
    for j in range(count):
        cols, here = block(j), block(start + j)
        remote, at = remotes[j]
        summed = held[:, here].astype(F32) + remote[:, block(at)].astype(F32)
        outer_grad = code(summed * 0.25, scales, start + j)
        moved = momentum_decay * momentum[:, here] + outer_grad
        value = base[:, here] - outer_rate * (outer_grad + momentum_decay * moved)
        moved_out[:, cols] = moved
        sent[:, cols] = value.astype(BF16)
        keep, at = kept[j]
        keep[:, block(at)] = value


def blend_kernel(parts, n_values, n_moved, n_held, local, share, *refs):
    values = refs[:n_values]
    moved = refs[n_values : n_values + n_moved]
    refs = refs[n_values + n_moved + n_held :]
    new_base, new_local = refs[:2]
    out_base, out_local, sems = refs[-3:]
    rep = lax.axis_index("rep")
    leaving = Copies(sems)
    outs = []
    if n_moved:
        for ref, (start, count) in zip(moved, cut(0, [ref.shape[1] // BLOCK for ref in moved])):
            outs.append(leaving.start(ref, refs[2].at[:, span(start, count)]))
    part = share[0:1, :]
    at = 0
    for value, (flip, start, count) in zip(values, parts):
        for i, n in pieces_of(count):
            for j in range(n):
                layer = local[0, :, window(rep ^ flip, start + i + j, 1)].astype(F32)
                arrived = value[:, block(i + j)].astype(F32)
                out_base[:, block(at + j)] = arrived.astype(BF16).astype(F32)
                out_local[:, block(at + j)] = (part * layer + (1.0 - part) * arrived).astype(BF16)
            cols, here = window(rep ^ flip, start + i, n), span(at, n)
            outs += [
                leaving.start(out_base.at[:, here], new_base.at[:, cols]),
                leaving.start(out_local.at[:, here], new_local.at[0, :, cols]),
            ]
            at += n
    for copy in outs:
        copy.wait()


def on_device(base_weights, local_weights, momentum, drift_exponent, sum_exponent, blend_ratio):
    rows, cols = base_weights.shape
    owned = momentum.shape[1]
    blocks = drift_exponent.shape[2]
    sum_exponent = jnp.pad(sum_exponent, ((0, 0), (0, BLOCK - sum_exponent.shape[1])))
    share = blend_ratio[0].astype(F32) / blend_ratio[1].astype(F32)
    share = jnp.full((8, BLOCK), share, F32)
    in_hbm = [
        pltpu.with_memory_space_constraint(x, pltpu.HBM)
        for x in (base_weights, local_weights, drift_exponent, momentum)
    ]

    def wide(count, dtype):
        return pltpu.VMEM((rows, count * BLOCK), dtype)

    def sems(n):
        return pltpu.SemaphoreType.DMA((n,))

    def some(count, dtype):
        return jax.ShapeDtypeStruct((rows, count * BLOCK), dtype)

    def call(body, in_specs, out_specs, out_shape, scratch, name, aliases=None):
        return pl.pallas_call(
            body,
            in_specs=in_specs,
            out_specs=out_specs,
            out_shape=out_shape,
            scratch_shapes=scratch,
            input_output_aliases=aliases or {},
            compiler_params=pltpu.CompilerParams(vmem_limit_bytes=VMEM_LIMIT),
            cost_estimate=pl.CostEstimate(flops=1, bytes_accessed=1, transcendentals=0),
            name=name,
        )

    def codes(parts, after=()):
        count = sum(p[2] for p in parts)
        n = sum(len(pieces_of(p[2])) for p in parts)
        return call(
            functools.partial(codes_kernel, parts, len(after)),
            [IN_HBM] * 3 + [ANYWHERE] * len(after), (IN_VMEM,) * len(parts),
            tuple(some(p[2], BF16) for p in parts),
            [wide(count, F32), wide(count, BF16), pltpu.VMEM((1, rows, blocks), jnp.int32), sems(1 + 2 * n)],
            "codes",
        )(*in_hbm[:3], *after)

    def pair(own, others):
        return call(
            pair_kernel, [IN_VMEM] * (1 + len(others)), IN_VMEM, jax.ShapeDtypeStruct(own.shape, BF16), [], "pair",
        )(own, *others)

    def prepare(others):
        n = 2 * len(pieces_of(QUARTER)) + 2
        return call(
            functools.partial(prepare_kernel, len(others)),
            [IN_HBM] * 4 + [IN_VMEM] * (1 + len(others)), (IN_VMEM,) * 5,
            (some(QUARTER, F32), some(QUARTER, F32), some(QUARTER, BF16), some(1, F32), some(1, F32)),
            [wide(QUARTER, BF16), pltpu.VMEM((1, rows, blocks), jnp.int32), sems(n)], "prepare",
        )(*in_hbm, sum_exponent, *others)

    def update(start, count, skip, prepared, remotes, near):
        sent, moved, *kept = call(
            functools.partial(update_kernel, start, count, skip, len(remotes)), [IN_VMEM] * (5 + len(remotes)), (IN_VMEM,) * (2 + len(near)),
            (some(count, BF16), some(count, F32), *(some(n, F32) for n in near)), [], "update",
        )(*prepared, *remotes)
        return sent, moved, kept

    full = (
        jax.ShapeDtypeStruct((rows, cols), F32),
        jax.ShapeDtypeStruct((1, rows, cols), BF16),
        jax.ShapeDtypeStruct((rows, owned), F32),
    )

    def blend(parts, values, held=(), moved=()):
        count = sum(p[2] for p in parts)
        n = sum(len(pieces_of(p[2])) for p in parts)
        n_out = 3 if moved else 2
        at = 2 + len(values) + len(moved)
        return call(
            functools.partial(blend_kernel, parts, len(values), len(moved), len(held)),
            [IN_VMEM] * at + [IN_HBM] * len(held), (IN_HBM,) * n_out, full[:n_out],
            [wide(count, F32), wide(count, BF16), sems(2 * n + len(moved))],
            "blend", {at + i: i for i in range(len(held))},
        )(local_weights, share, *values, *moved, *held)

    def to_core(x):
        return lax.ppermute(x, "rep", [(0, 1), (1, 0), (2, 3), (3, 2)])

    def to_chip(x):
        return lax.ppermute(x, "rep", [(0, 2), (2, 0), (1, 3), (3, 1)])

    first, second = cut(0, (FIRST, SECOND))
    (there_first,) = codes([(3, *first)])
    here_first, *there_second = codes([(2, *first)] + [(3, *part) for part in cut(FIRST, AWAY_SECOND)], (there_first,))
    pair_first = pair(here_first, [to_core(there_first)])
    here_second, *mine = codes([(2, *second)] + [(1, *part) for part in cut(0, CODES)], (pair_first,))
    others = [to_core(x) for x in mine]
    pair_second = pair(here_second, [to_core(x) for x in there_second])
    chip_first, chip_second = to_chip(pair_first), to_chip(pair_second)
    prepared = prepare(others)
    first, second = cut(0, (BACK_FIRST, BACK_SECOND))
    sent_first, moved_first, kept_first = update(*first, 0, prepared, (chip_first,), NEAR_FIRST)
    remotes, skip = ((chip_first, chip_second), BACK_FIRST) if BACK_FIRST < FIRST else ((chip_second,), 0)
    sent_second, moved_second, kept_second = update(*second, skip, prepared, remotes, NEAR_SECOND)
    far_first, far_second = to_chip(sent_first), to_chip(sent_second)
    kept = [*kept_first, *kept_second]
    near = [to_core(x) for x in kept]
    pieces = cut(0, NEAR_FIRST + NEAR_SECOND)
    *held, new_momentum = blend(
        [(0, *part) for part in pieces] + [(1, *part) for part in pieces], kept + near,
        moved=(moved_first, moved_second),
    )
    pieces = cut(0, FORWARD_FIRST)
    forwarded = [to_core(lax.slice_in_dim(far_first, at * BLOCK, (at + n) * BLOCK, axis=1)) for at, n in pieces]
    held = blend([(2, *first)] + [(3, *piece) for piece in pieces], [far_first] + forwarded, held)
    far_second, held = lax.optimization_barrier((far_second, held))
    forwarded = to_core(far_second)
    held = blend([(2, *second)], [far_second], held)
    new_base, new_local = blend([(3, *second)], [forwarded], held)
    return new_base, new_momentum, new_local


def solution(mesh):
    return jax.shard_map(
        on_device,
        mesh=mesh,
        in_specs=(
            P("fsdp", None),
            P("rep", "fsdp", None),
            P("fsdp", "rep"),
            P("rep", "fsdp", None),
            P("fsdp", "rep"),
            P(),
        ),
        out_specs=(P("fsdp", None), P("fsdp", "rep"), P("rep", "fsdp", None)),
        check_vma=False,
    )
```

```python
import functools

import jax
import jax.numpy as jnp
from jax import lax
from jax.experimental import pallas as pl
from jax.experimental.pallas import tpu as pltpu
from jax.sharding import PartitionSpec as P

BLOCK = 128
QUARTER = 28
FIRST, SECOND = 18, 10
BACK_FIRST, BACK_SECOND = 14, 14
AWAY_SECOND = (10,)
CODES = (10, 9, 9)
NEAR_FIRST, NEAR_SECOND = (7, 7), (5, 5, 4)
FORWARD_FIRST = (7, 7)
PIECE = 9
VMEM_LIMIT = 12 * 1024 * 1024

momentum_decay = 0.9
outer_rate = 0.7

F32 = jnp.float32
BF16 = jnp.bfloat16
IN_HBM = pl.BlockSpec(memory_space=pltpu.HBM)
ANYWHERE = pl.BlockSpec(memory_space=pl.ANY)
IN_VMEM = pl.BlockSpec(memory_space=pltpu.VMEM)


class Copies:
    def __init__(self, sems):
        self.sems = sems
        self.used = 0

    def start(self, source, target):
        copy = pltpu.make_async_copy(source, target, self.sems.at[self.used])
        self.used += 1
        copy.start()
        return copy


def pieces_of(blocks):
    return [(i, min(PIECE, blocks - i)) for i in range(0, blocks, PIECE)]


def cut(start, counts):
    return [(start + sum(counts[:i]), count) for i, count in enumerate(counts)]


def window(quarter, start, count):
    return pl.ds(pl.multiple_of((quarter * QUARTER + start) * BLOCK, BLOCK), count * BLOCK)


def span(start, count):
    return pl.ds(start * BLOCK, count * BLOCK)


def block(j):
    return slice(j * BLOCK, (j + 1) * BLOCK)


def places_in(refs):
    return [(ref, j) for ref in refs for j in range(ref.shape[1] // BLOCK)]


def scale_table(exponent):
    rows, blocks = exponent.shape
    if blocks < BLOCK:
        exponent = jnp.concatenate([exponent, jnp.zeros((rows, BLOCK - blocks), jnp.int32)], 1)
    scale = jnp.zeros(exponent.shape, F32)
    inverse = jnp.zeros(exponent.shape, F32)
    for value in range(-8, 1):
        hit = exponent == value
        scale = jnp.where(hit, F32(2.0**value), scale)
        inverse = jnp.where(hit, F32(2.0**-value), inverse)
    return scale, inverse


def rolled(table, first):
    return tuple(pltpu.roll(x, lax.rem(BLOCK - first, BLOCK), 1) for x in table)


def code(values, scales, j):
    scale, inverse = (s[:, j : j + 1] for s in scales)
    return jnp.clip(jnp.floor(values * inverse + 0.5), -8.0, 7.0) * scale


def codes_kernel(parts, n_after, base, local, drift, *refs):
    outs = refs[n_after : n_after + len(parts)]
    base_at, local_at, drift_at, sems = refs[n_after + len(parts) :]
    rep = lax.axis_index("rep")
    copies = Copies(sems)
    exps = copies.start(drift, drift_at)
    arriving = []
    at = 0
    for out, (flip, start, count) in zip(outs, parts):
        for i, n in pieces_of(count):
            cols, here = window(rep ^ flip, start + i, n), span(at, n)
            arriving.append((
                out, i, n, at, (rep ^ flip) * QUARTER + start + i,
                copies.start(base.at[:, cols], base_at.at[:, here]),
                copies.start(local.at[0, :, cols], local_at.at[:, here]),
            ))
            at += n
    exps.wait()
    table = scale_table(drift_at[0])
    for out, i, n, at, first, *group in arriving:
        scales = rolled(table, first)
        for copy in group:
            copy.wait()
        for j in range(n):
            cols = block(at + j)
            drifted = base_at[:, cols] - local_at[:, cols].astype(F32)
            out[:, block(i + j)] = code(drifted, scales, j).astype(BF16)


def pair_kernel(own, *refs):
    *others, out = refs
    for j, (other, at) in enumerate(places_in(others)):
        cols = block(j)
        out[:, cols] = (own[:, cols].astype(F32) + other[:, block(at)].astype(F32)).astype(BF16)


def prepare_kernel(n_others, base, local, drift, momentum, sums, *refs):
    others = places_in(refs[:n_others])
    base_out, momentum_out, held, scale_out, inverse_out, local_at, drift_at, sems = refs[n_others:]
    quarter = lax.axis_index("rep")
    copies = Copies(sems)
    exps = copies.start(drift, drift_at)
    arriving = []
    for i, n in pieces_of(QUARTER):
        cols, here = window(quarter, i, n), span(i, n)
        arriving.append((
            copies.start(base.at[:, cols], base_out.at[:, here]),
            copies.start(local.at[0, :, cols], local_at.at[:, here]),
        ))
    last = copies.start(momentum, momentum_out)
    scale_out[...], inverse_out[...] = scale_table(sums[...])
    exps.wait()
    scales = rolled(scale_table(drift_at[0]), quarter * QUARTER)
    for (i, n), group in zip(pieces_of(QUARTER), arriving):
        for copy in group:
            copy.wait()
        for j in range(i, i + n):
            cols = block(j)
            other, at = others[j]
            own = code(base_out[:, cols] - local_at[:, cols].astype(F32), scales, j)
            held[:, cols] = (own + other[:, block(at)].astype(F32)).astype(BF16)
    last.wait()


def update_kernel(start, count, skip, n_remote, base, momentum, held, scale, inverse, *refs):
    remotes = places_in(refs[:n_remote])[skip:]
    sent, moved_out, *kept = refs[n_remote:]
    kept = places_in(kept)
    scales = scale[...], inverse[...]
    for j in range(count):
        cols, here = block(j), block(start + j)
        remote, at = remotes[j]
        summed = held[:, here].astype(F32) + remote[:, block(at)].astype(F32)
        outer_grad = code(summed * 0.25, scales, start + j)
        moved = momentum_decay * momentum[:, here] + outer_grad
        value = base[:, here] - outer_rate * (outer_grad + momentum_decay * moved)
        moved_out[:, cols] = moved
        sent[:, cols] = value.astype(BF16)
        keep, at = kept[j]
        keep[:, block(at)] = value


def blend_kernel(parts, n_values, n_moved, n_held, local, share, *refs):
    values = refs[:n_values]
    moved = refs[n_values : n_values + n_moved]
    refs = refs[n_values + n_moved + n_held :]
    new_base, new_local = refs[:2]
    out_base, out_local, sems = refs[-3:]
    rep = lax.axis_index("rep")
    leaving = Copies(sems)
    outs = []
    if n_moved:
        for ref, (start, count) in zip(moved, cut(0, [ref.shape[1] // BLOCK for ref in moved])):
            outs.append(leaving.start(ref, refs[2].at[:, span(start, count)]))
    part = share[0:1, :]
    at = 0
    for value, (flip, start, count) in zip(values, parts):
        for i, n in pieces_of(count):
            for j in range(n):
                layer = local[0, :, window(rep ^ flip, start + i + j, 1)].astype(F32)
                arrived = value[:, block(i + j)].astype(F32)
                out_base[:, block(at + j)] = arrived.astype(BF16).astype(F32)
                out_local[:, block(at + j)] = (part * layer + (1.0 - part) * arrived).astype(BF16)
            cols, here = window(rep ^ flip, start + i, n), span(at, n)
            outs += [
                leaving.start(out_base.at[:, here], new_base.at[:, cols]),
                leaving.start(out_local.at[:, here], new_local.at[0, :, cols]),
            ]
            at += n
    for copy in outs:
        copy.wait()


def on_device(base_weights, local_weights, momentum, drift_exponent, sum_exponent, blend_ratio):
    rows, cols = base_weights.shape
    owned = momentum.shape[1]
    blocks = drift_exponent.shape[2]
    sum_exponent = jnp.pad(sum_exponent, ((0, 0), (0, BLOCK - sum_exponent.shape[1])))
    share = blend_ratio[0].astype(F32) / blend_ratio[1].astype(F32)
    share = jnp.full((8, BLOCK), share, F32)
    in_hbm = [
        pltpu.with_memory_space_constraint(x, pltpu.HBM)
        for x in (base_weights, local_weights, drift_exponent, momentum)
    ]

    def wide(count, dtype):
        return pltpu.VMEM((rows, count * BLOCK), dtype)

    def sems(n):
        return pltpu.SemaphoreType.DMA((n,))

    def some(count, dtype):
        return jax.ShapeDtypeStruct((rows, count * BLOCK), dtype)

    def call(body, in_specs, out_specs, out_shape, scratch, name, aliases=None):
        return pl.pallas_call(
            body,
            in_specs=in_specs,
            out_specs=out_specs,
            out_shape=out_shape,
            scratch_shapes=scratch,
            input_output_aliases=aliases or {},
            compiler_params=pltpu.CompilerParams(vmem_limit_bytes=VMEM_LIMIT),
            cost_estimate=pl.CostEstimate(flops=1, bytes_accessed=1, transcendentals=0),
            name=name,
        )

    def codes(parts, after=()):
        count = sum(p[2] for p in parts)
        n = sum(len(pieces_of(p[2])) for p in parts)
        return call(
            functools.partial(codes_kernel, parts, len(after)),
            [IN_HBM] * 3 + [ANYWHERE] * len(after), (IN_VMEM,) * len(parts),
            tuple(some(p[2], BF16) for p in parts),
            [wide(count, F32), wide(count, BF16), pltpu.VMEM((1, rows, blocks), jnp.int32), sems(1 + 2 * n)],
            "codes",
        )(*in_hbm[:3], *after)

    def pair(own, others):
        return call(
            pair_kernel, [IN_VMEM] * (1 + len(others)), IN_VMEM, jax.ShapeDtypeStruct(own.shape, BF16), [], "pair",
        )(own, *others)

    def prepare(others):
        n = 2 * len(pieces_of(QUARTER)) + 2
        return call(
            functools.partial(prepare_kernel, len(others)),
            [IN_HBM] * 4 + [IN_VMEM] * (1 + len(others)), (IN_VMEM,) * 5,
            (some(QUARTER, F32), some(QUARTER, F32), some(QUARTER, BF16), some(1, F32), some(1, F32)),
            [wide(QUARTER, BF16), pltpu.VMEM((1, rows, blocks), jnp.int32), sems(n)], "prepare",
        )(*in_hbm, sum_exponent, *others)

    def update(start, count, skip, prepared, remotes, near):
        sent, moved, *kept = call(
            functools.partial(update_kernel, start, count, skip, len(remotes)), [IN_VMEM] * (5 + len(remotes)), (IN_VMEM,) * (2 + len(near)),
            (some(count, BF16), some(count, F32), *(some(n, F32) for n in near)), [], "update",
        )(*prepared, *remotes)
        return sent, moved, kept

    full = (
        jax.ShapeDtypeStruct((rows, cols), F32),
        jax.ShapeDtypeStruct((1, rows, cols), BF16),
        jax.ShapeDtypeStruct((rows, owned), F32),
    )

    def blend(parts, values, held=(), moved=()):
        count = sum(p[2] for p in parts)
        n = sum(len(pieces_of(p[2])) for p in parts)
        n_out = 3 if moved else 2
        at = 2 + len(values) + len(moved)
        return call(
            functools.partial(blend_kernel, parts, len(values), len(moved), len(held)),
            [IN_VMEM] * at + [IN_HBM] * len(held), (IN_HBM,) * n_out, full[:n_out],
            [wide(count, F32), wide(count, BF16), sems(2 * n + len(moved))],
            "blend", {at + i: i for i in range(len(held))},
        )(local_weights, share, *values, *moved, *held)

    def to_core(x):
        return lax.ppermute(x, "rep", [(0, 1), (1, 0), (2, 3), (3, 2)])

    def to_chip(x):
        return lax.ppermute(x, "rep", [(0, 2), (2, 0), (1, 3), (3, 1)])

    first, second = cut(0, (FIRST, SECOND))
    (there_first,) = codes([(3, *first)])
    here_first, *there_second = codes([(2, *first)] + [(3, *part) for part in cut(FIRST, AWAY_SECOND)], (there_first,))
    pair_first = pair(here_first, [to_core(there_first)])
    here_second, *mine = codes([(2, *second)] + [(1, *part) for part in cut(0, CODES)], (pair_first,))
    others = [to_core(x) for x in mine]
    pair_second = pair(here_second, [to_core(x) for x in there_second])
    chip_first, chip_second = to_chip(pair_first), to_chip(pair_second)
    prepared = prepare(others)
    first, second = cut(0, (BACK_FIRST, BACK_SECOND))
    sent_first, moved_first, kept_first = update(*first, 0, prepared, (chip_first,), NEAR_FIRST)
    remotes, skip = ((chip_first, chip_second), BACK_FIRST) if BACK_FIRST < FIRST else ((chip_second,), 0)
    sent_second, moved_second, kept_second = update(*second, skip, prepared, remotes, NEAR_SECOND)
    far_first, far_second = to_chip(sent_first), to_chip(sent_second)
    kept = [*kept_first, *kept_second]
    near = [to_core(x) for x in kept]
    pieces = cut(0, NEAR_FIRST + NEAR_SECOND)
    *held, new_momentum = blend(
        [(0, *part) for part in pieces] + [(1, *part) for part in pieces], kept + near,
        moved=(moved_first, moved_second),
    )
    pieces = cut(0, FORWARD_FIRST)
    forwarded = [to_core(lax.slice_in_dim(far_first, at * BLOCK, (at + n) * BLOCK, axis=1)) for at, n in pieces]
    held = blend([(2, *first)] + [(3, *piece) for piece in pieces], [far_first] + forwarded, held)
    far_second, held = lax.optimization_barrier((far_second, held))
    forwarded = to_core(far_second)
    held = blend([(2, *second)], [far_second], held)
    new_base, new_local = blend([(3, *second)], [forwarded], held)
    return new_base, new_momentum, new_local


def solution(mesh):
    return jax.shard_map(
        on_device,
        mesh=mesh,
        in_specs=(
            P("fsdp", None),
            P("rep", "fsdp", None),
            P("fsdp", "rep"),
            P("rep", "fsdp", None),
            P("fsdp", "rep"),
            P(),
        ),
        out_specs=(P("fsdp", None), P("fsdp", "rep"), P("rep", "fsdp", None)),
        check_vma=False,
    )
```

```python
import functools

import jax
import jax.numpy as jnp
from jax import lax
from jax.experimental import pallas as pl
from jax.experimental.pallas import tpu as pltpu
from jax.sharding import PartitionSpec as P

BLOCK = 128
QUARTER = 28
FIRST, SECOND = 18, 10
BACK_FIRST, BACK_SECOND = 14, 14
AWAY_SECOND = (10,)
CODES = (12, 8, 8)
NEAR_FIRST, NEAR_SECOND = (8, 6), (5, 5, 4)
FORWARD_FIRST = (7, 7)
PIECE = 9
VMEM_LIMIT = 12 * 1024 * 1024

momentum_decay = 0.9
outer_rate = 0.7

F32 = jnp.float32
BF16 = jnp.bfloat16
IN_HBM = pl.BlockSpec(memory_space=pltpu.HBM)
ANYWHERE = pl.BlockSpec(memory_space=pl.ANY)
IN_VMEM = pl.BlockSpec(memory_space=pltpu.VMEM)


class Copies:
    def __init__(self, sems):
        self.sems = sems
        self.used = 0

    def start(self, source, target):
        copy = pltpu.make_async_copy(source, target, self.sems.at[self.used])
        self.used += 1
        copy.start()
        return copy


def pieces_of(blocks):
    return [(i, min(PIECE, blocks - i)) for i in range(0, blocks, PIECE)]


def cut(start, counts):
    return [(start + sum(counts[:i]), count) for i, count in enumerate(counts)]


def window(quarter, start, count):
    return pl.ds(pl.multiple_of((quarter * QUARTER + start) * BLOCK, BLOCK), count * BLOCK)


def span(start, count):
    return pl.ds(start * BLOCK, count * BLOCK)


def block(j):
    return slice(j * BLOCK, (j + 1) * BLOCK)


def places_in(refs):
    return [(ref, j) for ref in refs for j in range(ref.shape[1] // BLOCK)]


def scale_table(exponent):
    rows, blocks = exponent.shape
    if blocks < BLOCK:
        exponent = jnp.concatenate([exponent, jnp.zeros((rows, BLOCK - blocks), jnp.int32)], 1)
    scale = jnp.zeros(exponent.shape, F32)
    inverse = jnp.zeros(exponent.shape, F32)
    for value in range(-8, 1):
        hit = exponent == value
        scale = jnp.where(hit, F32(2.0**value), scale)
        inverse = jnp.where(hit, F32(2.0**-value), inverse)
    return scale, inverse


def rolled(table, first):
    return tuple(pltpu.roll(x, lax.rem(BLOCK - first, BLOCK), 1) for x in table)


def code(values, scales, j):
    scale, inverse = (s[:, j : j + 1] for s in scales)
    return jnp.clip(jnp.floor(values * inverse + 0.5), -8.0, 7.0) * scale


def codes_kernel(parts, n_after, base, local, drift, *refs):
    outs = refs[n_after : n_after + len(parts)]
    base_at, local_at, drift_at, sems = refs[n_after + len(parts) :]
    rep = lax.axis_index("rep")
    copies = Copies(sems)
    exps = copies.start(drift, drift_at)
    arriving = []
    at = 0
    for out, (flip, start, count) in zip(outs, parts):
        for i, n in pieces_of(count):
            cols, here = window(rep ^ flip, start + i, n), span(at, n)
            arriving.append((
                out, i, n, at, (rep ^ flip) * QUARTER + start + i,
                copies.start(base.at[:, cols], base_at.at[:, here]),
                copies.start(local.at[0, :, cols], local_at.at[:, here]),
            ))
            at += n
    exps.wait()
    table = scale_table(drift_at[0])
    for out, i, n, at, first, *group in arriving:
        scales = rolled(table, first)
        for copy in group:
            copy.wait()
        for j in range(n):
            cols = block(at + j)
            drifted = base_at[:, cols] - local_at[:, cols].astype(F32)
            out[:, block(i + j)] = code(drifted, scales, j).astype(BF16)


def pair_kernel(own, *refs):
    *others, out = refs
    for j, (other, at) in enumerate(places_in(others)):
        cols = block(j)
        out[:, cols] = (own[:, cols].astype(F32) + other[:, block(at)].astype(F32)).astype(BF16)


def prepare_kernel(n_others, base, local, drift, momentum, sums, *refs):
    others = places_in(refs[:n_others])
    base_out, momentum_out, held, scale_out, inverse_out, local_at, drift_at, sems = refs[n_others:]
    quarter = lax.axis_index("rep")
    copies = Copies(sems)
    exps = copies.start(drift, drift_at)
    arriving = []
    for i, n in pieces_of(QUARTER):
        cols, here = window(quarter, i, n), span(i, n)
        arriving.append((
            copies.start(base.at[:, cols], base_out.at[:, here]),
            copies.start(local.at[0, :, cols], local_at.at[:, here]),
        ))
    last = copies.start(momentum, momentum_out)
    scale_out[...], inverse_out[...] = scale_table(sums[...])
    exps.wait()
    scales = rolled(scale_table(drift_at[0]), quarter * QUARTER)
    for (i, n), group in zip(pieces_of(QUARTER), arriving):
        for copy in group:
            copy.wait()
        for j in range(i, i + n):
            cols = block(j)
            other, at = others[j]
            own = code(base_out[:, cols] - local_at[:, cols].astype(F32), scales, j)
            held[:, cols] = (own + other[:, block(at)].astype(F32)).astype(BF16)
    last.wait()


def update_kernel(start, count, skip, n_remote, base, momentum, held, scale, inverse, *refs):
    remotes = places_in(refs[:n_remote])[skip:]
    sent, moved_out, *kept = refs[n_remote:]
    kept = places_in(kept)
    scales = scale[...], inverse[...]
    for j in range(count):
        cols, here = block(j), block(start + j)
        remote, at = remotes[j]
        summed = held[:, here].astype(F32) + remote[:, block(at)].astype(F32)
        outer_grad = code(summed * 0.25, scales, start + j)
        moved = momentum_decay * momentum[:, here] + outer_grad
        value = base[:, here] - outer_rate * (outer_grad + momentum_decay * moved)
        moved_out[:, cols] = moved
        sent[:, cols] = value.astype(BF16)
        keep, at = kept[j]
        keep[:, block(at)] = value


def blend_kernel(parts, n_values, n_moved, n_held, local, share, *refs):
    values = refs[:n_values]
    moved = refs[n_values : n_values + n_moved]
    refs = refs[n_values + n_moved + n_held :]
    new_base, new_local = refs[:2]
    out_base, out_local, sems = refs[-3:]
    rep = lax.axis_index("rep")
    leaving = Copies(sems)
    outs = []
    if n_moved:
        for ref, (start, count) in zip(moved, cut(0, [ref.shape[1] // BLOCK for ref in moved])):
            outs.append(leaving.start(ref, refs[2].at[:, span(start, count)]))
    part = share[0:1, :]
    at = 0
    for value, (flip, start, count) in zip(values, parts):
        for i, n in pieces_of(count):
            for j in range(n):
                layer = local[0, :, window(rep ^ flip, start + i + j, 1)].astype(F32)
                arrived = value[:, block(i + j)].astype(F32)
                out_base[:, block(at + j)] = arrived.astype(BF16).astype(F32)
                out_local[:, block(at + j)] = (part * layer + (1.0 - part) * arrived).astype(BF16)
            cols, here = window(rep ^ flip, start + i, n), span(at, n)
            outs += [
                leaving.start(out_base.at[:, here], new_base.at[:, cols]),
                leaving.start(out_local.at[:, here], new_local.at[0, :, cols]),
            ]
            at += n
    for copy in outs:
        copy.wait()


def on_device(base_weights, local_weights, momentum, drift_exponent, sum_exponent, blend_ratio):
    rows, cols = base_weights.shape
    owned = momentum.shape[1]
    blocks = drift_exponent.shape[2]
    sum_exponent = jnp.pad(sum_exponent, ((0, 0), (0, BLOCK - sum_exponent.shape[1])))
    share = blend_ratio[0].astype(F32) / blend_ratio[1].astype(F32)
    share = jnp.full((8, BLOCK), share, F32)
    in_hbm = [
        pltpu.with_memory_space_constraint(x, pltpu.HBM)
        for x in (base_weights, local_weights, drift_exponent, momentum)
    ]

    def wide(count, dtype):
        return pltpu.VMEM((rows, count * BLOCK), dtype)

    def sems(n):
        return pltpu.SemaphoreType.DMA((n,))

    def some(count, dtype):
        return jax.ShapeDtypeStruct((rows, count * BLOCK), dtype)

    def call(body, in_specs, out_specs, out_shape, scratch, name, aliases=None):
        return pl.pallas_call(
            body,
            in_specs=in_specs,
            out_specs=out_specs,
            out_shape=out_shape,
            scratch_shapes=scratch,
            input_output_aliases=aliases or {},
            compiler_params=pltpu.CompilerParams(vmem_limit_bytes=VMEM_LIMIT),
            cost_estimate=pl.CostEstimate(flops=1, bytes_accessed=1, transcendentals=0),
            name=name,
        )

    def codes(parts, after=()):
        count = sum(p[2] for p in parts)
        n = sum(len(pieces_of(p[2])) for p in parts)
        return call(
            functools.partial(codes_kernel, parts, len(after)),
            [IN_HBM] * 3 + [ANYWHERE] * len(after), (IN_VMEM,) * len(parts),
            tuple(some(p[2], BF16) for p in parts),
            [wide(count, F32), wide(count, BF16), pltpu.VMEM((1, rows, blocks), jnp.int32), sems(1 + 2 * n)],
            "codes",
        )(*in_hbm[:3], *after)

    def pair(own, others):
        return call(
            pair_kernel, [IN_VMEM] * (1 + len(others)), IN_VMEM, jax.ShapeDtypeStruct(own.shape, BF16), [], "pair",
        )(own, *others)

    def prepare(others):
        n = 2 * len(pieces_of(QUARTER)) + 2
        return call(
            functools.partial(prepare_kernel, len(others)),
            [IN_HBM] * 4 + [IN_VMEM] * (1 + len(others)), (IN_VMEM,) * 5,
            (some(QUARTER, F32), some(QUARTER, F32), some(QUARTER, BF16), some(1, F32), some(1, F32)),
            [wide(QUARTER, BF16), pltpu.VMEM((1, rows, blocks), jnp.int32), sems(n)], "prepare",
        )(*in_hbm, sum_exponent, *others)

    def update(start, count, skip, prepared, remotes, near):
        sent, moved, *kept = call(
            functools.partial(update_kernel, start, count, skip, len(remotes)), [IN_VMEM] * (5 + len(remotes)), (IN_VMEM,) * (2 + len(near)),
            (some(count, BF16), some(count, F32), *(some(n, F32) for n in near)), [], "update",
        )(*prepared, *remotes)
        return sent, moved, kept

    full = (
        jax.ShapeDtypeStruct((rows, cols), F32),
        jax.ShapeDtypeStruct((1, rows, cols), BF16),
        jax.ShapeDtypeStruct((rows, owned), F32),
    )

    def blend(parts, values, held=(), moved=()):
        count = sum(p[2] for p in parts)
        n = sum(len(pieces_of(p[2])) for p in parts)
        n_out = 3 if moved else 2
        at = 2 + len(values) + len(moved)
        return call(
            functools.partial(blend_kernel, parts, len(values), len(moved), len(held)),
            [IN_VMEM] * at + [IN_HBM] * len(held), (IN_HBM,) * n_out, full[:n_out],
            [wide(count, F32), wide(count, BF16), sems(2 * n + len(moved))],
            "blend", {at + i: i for i in range(len(held))},
        )(local_weights, share, *values, *moved, *held)

    def to_core(x):
        return lax.ppermute(x, "rep", [(0, 1), (1, 0), (2, 3), (3, 2)])

    def to_chip(x):
        return lax.ppermute(x, "rep", [(0, 2), (2, 0), (1, 3), (3, 1)])

    first, second = cut(0, (FIRST, SECOND))
    (there_first,) = codes([(3, *first)])
    here_first, *there_second = codes([(2, *first)] + [(3, *part) for part in cut(FIRST, AWAY_SECOND)], (there_first,))
    pair_first = pair(here_first, [to_core(there_first)])
    here_second, *mine = codes([(2, *second)] + [(1, *part) for part in cut(0, CODES)], (pair_first,))
    others = [to_core(x) for x in mine]
    pair_second = pair(here_second, [to_core(x) for x in there_second])
    chip_first, chip_second = to_chip(pair_first), to_chip(pair_second)
    prepared = prepare(others)
    first, second = cut(0, (BACK_FIRST, BACK_SECOND))
    sent_first, moved_first, kept_first = update(*first, 0, prepared, (chip_first,), NEAR_FIRST)
    remotes, skip = ((chip_first, chip_second), BACK_FIRST) if BACK_FIRST < FIRST else ((chip_second,), 0)
    sent_second, moved_second, kept_second = update(*second, skip, prepared, remotes, NEAR_SECOND)
    far_first, far_second = to_chip(sent_first), to_chip(sent_second)
    kept = [*kept_first, *kept_second]
    near = [to_core(x) for x in kept]
    pieces = cut(0, NEAR_FIRST + NEAR_SECOND)
    *held, new_momentum = blend(
        [(0, *part) for part in pieces] + [(1, *part) for part in pieces], kept + near,
        moved=(moved_first, moved_second),
    )
    pieces = cut(0, FORWARD_FIRST)
    forwarded = [to_core(lax.slice_in_dim(far_first, at * BLOCK, (at + n) * BLOCK, axis=1)) for at, n in pieces]
    held = blend([(2, *first)] + [(3, *piece) for piece in pieces], [far_first] + forwarded, held)
    far_second, held = lax.optimization_barrier((far_second, held))
    forwarded = to_core(far_second)
    held = blend([(2, *second)], [far_second], held)
    new_base, new_local = blend([(3, *second)], [forwarded], held)
    return new_base, new_momentum, new_local


def solution(mesh):
    return jax.shard_map(
        on_device,
        mesh=mesh,
        in_specs=(
            P("fsdp", None),
            P("rep", "fsdp", None),
            P("fsdp", "rep"),
            P("rep", "fsdp", None),
            P("fsdp", "rep"),
            P(),
        ),
        out_specs=(P("fsdp", None), P("fsdp", "rep"), P("rep", "fsdp", None)),
        check_vma=False,
    )
```
